1024 devices in a mesh: node: 32 (over z), inner: 4 (over y), rep: 8 (over x, core).
Axes of the slice: x: 4, y: 4, z: 32, core: 2. Of those that a mesh axis runs over, the one named last changes fastest.
Arguments:
- tokens: bfloat16 [16384, 1024], P(('node', 'inner', 'rep')), may hold values from -6 to 6
- out_grad: bfloat16 [16384, 1024], P(('node', 'inner', 'rep')), may hold values from -6 to 6
- expert_ids: int32 [16384, 10], P(('node', 'inner', 'rep')), may hold values from 0 to 255, as said below
- route_weight: float32 [16384, 10], P(('node', 'inner', 'rep')), may hold values from 0.1 to 0.6
- gate_weight: bfloat16 [256, 1024, 256], P(('node', 'inner')), may hold values from -0.1875 to 0.1875
- up_weight: bfloat16 [256, 1024, 256], P(('node', 'inner')), may hold values from -0.1875 to 0.1875
- down_weight: bfloat16 [256, 256, 1024], P(('node', 'inner')), may hold values from -0.375 to 0.375
Outputs:
- mixed: bfloat16 [16384, 1024], P(('node', 'inner', 'rep'))
- grad_tokens: bfloat16 [16384, 1024], P(('node', 'inner', 'rep'))
- grad_route: float32 [16384, 10], P(('node', 'inner', 'rep'))
- grad_gate: bfloat16 [256, 1024, 256], P(('node', 'inner'), 'rep')
- grad_up: bfloat16 [256, 1024, 256], P(('node', 'inner'), 'rep')
- grad_down: bfloat16 [256, 256, 1024], P(('node', 'inner'), None, 'rep')
The draws below stay inside these ranges and needn't reach their ends.
Inputs may be any that keep to these rules, and one draw needn't show every extreme that they name: `expert_ids`: each token names 10 different experts. Expert e is held in every rep group by the device whose index over node+inner is e // 2. The 160 entries of one device name experts of any one device at most 2 times and any one expert at most 1 times; every device names some device exactly 2 times and some expert exactly 1 times.
All inputs are finite; a program needn't handle non-finite values.
Results may differ from the reference program's by a relative error of at most 0.017.
Values may be sent and summed in bfloat16 or wider, within the bound.
A program may use at most 32 MiB of HBM per device.

```python
import jax
import jax.numpy as jnp
from jax import lax

D = 1024
FF = 256
TOP = 10
EXP_DEV = 2
TOK_DEV = 16
EXPERTS = 256
TOKENS = 16384
CAP = 2
ECAP = 1
N_NODE = 32
N_INNER = 4
N_REP = 8


def draw_expert_ids(key, part):
    key = jax.random.fold_in(key, 7)
    key_noise, key_hot, key_pick = jax.random.split(key, 3)
    device_count = EXPERTS // EXP_DEV
    block_count = TOKENS // TOK_DEV
    row_count = TOK_DEV * TOP
    used_count = (row_count + CAP - 1) // CAP
    noise = jax.random.randint(key_noise, (block_count, device_count), 0, 1 << 20)
    hottest = jax.random.randint(key_hot, (2,), 0, device_count)
    device_iota = jnp.arange(device_count, dtype=jnp.int32)
    is_hot = jnp.any(device_iota[:, None] == hottest[None, :], axis=1)
    scores = (noise + jnp.where(is_hot, 1 << 21, 0)) * device_count + device_iota[None, :]
    ranking = jnp.argsort(-scores, axis=1, stable=True).astype(jnp.int32)
    row_iota = jnp.arange(row_count, dtype=jnp.int32)
    position = row_iota % used_count
    occurrence = row_iota // used_count
    target = ranking[:, position]
    flips = jax.random.randint(key_pick, (block_count, used_count), 0, 2)
    local_pick = (occurrence[None, :] + flips[:, position]) % 2
    expert_rows = target * EXP_DEV + local_pick
    return expert_rows.reshape(TOKENS, TOP).astype(jnp.int32)


def shard_levels(rng, extent, pieces, low, largest):
    loudness = 1.0
    for dim, blocks in pieces:
        draws = jax.random.uniform(jax.random.fold_in(jax.random.fold_in(rng, 6), dim), (blocks,), jnp.float32, low / len(pieces), largest / len(pieces))
        loudness = loudness * jnp.repeat(jnp.exp(draws), extent[dim] // blocks).reshape((-1,) + (1,) * (len(extent) - 1 - dim))
    return loudness


def scatter_about(rng, extent, deviation, reach, cuts=(), held_as=jnp.bfloat16):
    entries = deviation * jax.random.normal(rng, extent, jnp.float32)
    if cuts:
        entries = entries * shard_levels(rng, extent, cuts, -0.22, 0.18)
    return jnp.clip(entries, -reach, reach).astype(held_as)


def setup_inputs(seed: int = 0) -> dict:
    seeds = jax.random.split(jax.random.key(seed), 8)
    return {
        "tokens": scatter_about(seeds[0], (TOKENS, D), 1.0, 6.0, ((0, 1024),)),
        "out_grad": scatter_about(seeds[1], (TOKENS, D), 1.0, 6.0, ((0, 1024),)),
        "expert_ids": draw_expert_ids(jax.random.fold_in(seeds[7], 71), 0),
        "route_weight": jnp.clip(0.1 + 0.5 * jax.random.uniform(seeds[3], (TOKENS, TOP), jnp.float32) ** shard_levels(seeds[3], (TOKENS, TOP), ((0, 1024),), -0.2, 0.2), 0.1, 0.6),
        "gate_weight": scatter_about(seeds[4], (EXPERTS, D, FF), D ** -0.5, 0.1875, ((0, 128),)),
        "up_weight": scatter_about(seeds[5], (EXPERTS, D, FF), D ** -0.5, 0.1875, ((0, 128),)),
        "down_weight": scatter_about(seeds[6], (EXPERTS, FF, D), FF ** -0.5, 0.375, ((0, 128),)),
    }


def settle(part):
    rounded = lax.optimization_barrier(part.astype(jnp.bfloat16))
    return jnp.sum(rounded.astype(jnp.float32), axis=0).astype(jnp.bfloat16)


def reference(tokens, out_grad, expert_ids, route_weight, gate_weight, up_weight, down_weight):
    slot_count = N_NODE * N_INNER * ECAP
    flat_ids = expert_ids.reshape(-1)
    flat_group = ((jnp.arange(TOKENS * TOP, dtype=jnp.int32) // TOP) // TOK_DEV) % N_REP
    flat_weight = route_weight.reshape(-1)
    groups = jnp.arange(N_REP, dtype=jnp.int32)

    def one_expert(running, expert):
        mixed_acc, token_acc, route_acc = running

        def pick_rows(group_index):
            chosen = (flat_ids == expert) & (flat_group == group_index)
            where_rows = jnp.nonzero(chosen, size=slot_count, fill_value=0)[0].astype(jnp.int32)
            is_valid = jnp.arange(slot_count, dtype=jnp.int32) < jnp.sum(chosen.astype(jnp.int32))
            return where_rows, is_valid

        entry_index, is_valid = jax.vmap(pick_rows)(groups)
        validity = is_valid.astype(jnp.float32)
        owner_token = entry_index // TOP
        inputs = tokens[owner_token].astype(jnp.float32)
        cotangent = out_grad[owner_token].astype(jnp.float32)
        weight_rows = flat_weight[entry_index] * validity
        w_gate = gate_weight[expert].astype(jnp.float32)
        w_up = up_weight[expert].astype(jnp.float32)
        w_down = down_weight[expert].astype(jnp.float32)
        gate_pre = jnp.einsum("gsd,df->gsf", inputs, w_gate)
        up_pre = jnp.einsum("gsd,df->gsf", inputs, w_up)
        gate_sig = jax.nn.sigmoid(gate_pre)
        silu_value = gate_pre * gate_sig
        activation = (silu_value * up_pre).astype(jnp.bfloat16)
        expert_out = jnp.einsum("gsf,fd->gsd", activation.astype(jnp.float32), w_down).astype(jnp.bfloat16)
        out_float = expert_out.astype(jnp.float32)
        flat_owner = owner_token.reshape(-1)
        mixed_acc = mixed_acc.at[flat_owner].add((weight_rows[:, :, None] * out_float).reshape(-1, D))
        route_part = jnp.sum(cotangent * out_float, axis=-1) * validity
        route_acc = route_acc.at[entry_index.reshape(-1)].add(route_part.reshape(-1))
        scaled = (weight_rows[:, :, None] * cotangent).astype(jnp.bfloat16)
        scaled_float = scaled.astype(jnp.float32)
        act_grad = jnp.einsum("gsd,fd->gsf", scaled_float, w_down)
        up_grad = (act_grad * silu_value).astype(jnp.bfloat16)
        gate_grad = (act_grad * up_pre * (gate_sig * (1.0 + gate_pre * (1.0 - gate_sig)))).astype(jnp.bfloat16)
        gate_float = gate_grad.astype(jnp.float32)
        up_float = up_grad.astype(jnp.float32)
        token_part = (jnp.einsum("gsf,df->gsd", gate_float, w_gate) + jnp.einsum("gsf,df->gsd", up_float, w_up)).astype(jnp.bfloat16)
        token_acc = token_acc.at[flat_owner].add(token_part.astype(jnp.float32).reshape(-1, D))
        part_gate = jnp.einsum("gsd,gsf->gdf", inputs, gate_float)
        part_up = jnp.einsum("gsd,gsf->gdf", inputs, up_float)
        part_down = jnp.einsum("gsf,gsd->gfd", activation.astype(jnp.float32), scaled_float)
        return (mixed_acc, token_acc, route_acc), (settle(part_gate), settle(part_up), settle(part_down))

    starting = (jnp.zeros((TOKENS, D), jnp.float32), jnp.zeros((TOKENS, D), jnp.float32), jnp.zeros((TOKENS * TOP,), jnp.float32))
    final, stacked = lax.scan(one_expert, starting, jnp.arange(EXPERTS, dtype=jnp.int32))
    mixed_acc, token_acc, route_acc = final
    grad_gate, grad_up, grad_down = stacked
    return (mixed_acc.astype(jnp.bfloat16), token_acc.astype(jnp.bfloat16), route_acc.reshape(TOKENS, TOP), grad_gate, grad_up, grad_down)
```

```python
import jax
import jax.numpy as jnp
from jax import lax
from jax.sharding import PartitionSpec as P

BF16 = jnp.bfloat16
F32 = jnp.float32
LANES = 128


def split_weight(weight):
    high = lax.reduce_precision(weight, 8, 7)
    rest = weight - high
    middle = lax.reduce_precision(rest, 8, 7)
    return high, middle, rest - middle


def per_device(tokens, out_grad, expert_ids, route_weight, gate_weight, up_weight, down_weight):
    token_count, width = tokens.shape
    top = expert_ids.shape[1]
    local = gate_weight.shape[0]
    nodes = lax.axis_size("node")
    inners = lax.axis_size("inner")
    node = lax.axis_index("node")
    inner = lax.axis_index("inner")
    meta = jnp.concatenate(
        (expert_ids.astype(F32),) + split_weight(route_weight)
        + (jnp.zeros((token_count, LANES - 4 * top), F32),),
        axis=1,
    ).astype(BF16)
    payload = jnp.concatenate((tokens, out_grad, meta), axis=1)
    gathered = lax.all_gather(payload, "node", axis=0, tiled=True)
    ids = gathered[:, 2 * width : 2 * width + top].astype(F32)
    plane = (node * (inners * local) + jnp.arange(inners * local, dtype=jnp.int32)).astype(F32)
    chosen = jnp.any(ids[None] == plane[:, None, None], axis=2).astype(BF16)
    pick = (
        chosen.reshape(inners * local, 1, nodes, token_count)
        * jnp.eye(nodes, dtype=BF16)[None, :, :, None]
    ).reshape(inners * local * nodes, nodes * token_count)
    slots = jnp.dot(pick, gathered, preferred_element_type=F32).astype(BF16)
    served = lax.all_to_all(
        slots.reshape(inners, local, nodes, -1), "inner", split_axis=0, concat_axis=0, tiled=True
    )
    served = served.transpose(1, 0, 2, 3).reshape(local, inners * nodes, -1)
    rows = served[:, :, :width]
    grads = served[:, :, width : 2 * width].astype(F32)
    extra = served[:, :, 2 * width :].astype(F32)
    mine = ((node * inners + inner) * local + jnp.arange(local, dtype=jnp.int32)).astype(F32)
    is_mine = (extra[:, :, :top] == mine[:, None, None]).astype(F32)
    weights = (
        extra[:, :, top : 2 * top] + extra[:, :, 2 * top : 3 * top] + extra[:, :, 3 * top : 4 * top]
    )
    weight = jnp.sum(weights * is_mine, axis=2, keepdims=True)
    scaled = (weight * grads).astype(BF16)
    gate_pre = jnp.einsum("esd,edf->esf", rows, gate_weight, preferred_element_type=F32)
    up_pre = jnp.einsum("esd,edf->esf", rows, up_weight, preferred_element_type=F32)
    gate_sig = jax.nn.sigmoid(gate_pre)
    silu = gate_pre * gate_sig
    activation = (silu * up_pre).astype(BF16)
    expert_out = jnp.einsum("esf,efd->esd", activation, down_weight, preferred_element_type=F32)
    act_grad = jnp.einsum("esd,efd->esf", scaled, down_weight, preferred_element_type=F32)
    up_grad = (act_grad * silu).astype(BF16)
    gate_grad = (act_grad * up_pre * (gate_sig * (1.0 + gate_pre * (1.0 - gate_sig)))).astype(BF16)
    back = jnp.einsum("esf,edf->esd", gate_grad, gate_weight, preferred_element_type=F32)
    back = back + jnp.einsum("esf,edf->esd", up_grad, up_weight, preferred_element_type=F32)
    route = jnp.sum(grads * expert_out, axis=2, keepdims=True) * is_mine
    route = jnp.pad(route, ((0, 0), (0, 0), (0, LANES - top)))
    answer = jnp.concatenate((weight * expert_out, back, route), axis=2).astype(BF16)
    answer = answer.reshape(local, inners, nodes, -1).transpose(1, 0, 2, 3)
    answer = lax.all_to_all(answer, "inner", split_axis=0, concat_axis=0, tiled=True)
    partial = jnp.einsum(
        "st,sd->td",
        pick,
        answer.reshape(inners * local * nodes, -1),
        preferred_element_type=F32,
    ).astype(BF16)
    total = lax.psum_scatter(partial, "node", scatter_dimension=0, tiled=True)
    term_gate = jnp.einsum("esd,esf->edf", rows, gate_grad, preferred_element_type=F32)
    term_up = jnp.einsum("esd,esf->edf", rows, up_grad, preferred_element_type=F32)
    term_down = jnp.einsum("esf,esd->efd", activation, scaled, preferred_element_type=F32)
    sum_gate = lax.psum_scatter(term_gate.astype(BF16), "rep", scatter_dimension=1, tiled=True)
    sum_up = lax.psum_scatter(term_up.astype(BF16), "rep", scatter_dimension=1, tiled=True)
    sum_down = lax.psum_scatter(term_down.astype(BF16), "rep", scatter_dimension=2, tiled=True)
    return (
        total[:, :width],
        total[:, width : 2 * width],
        total[:, 2 * width : 2 * width + top].astype(F32),
        sum_gate,
        sum_up,
        sum_down,
    )


def solution(mesh):
    split = P(("node", "inner", "rep"), None)
    held = P(("node", "inner"), None, None)
    return jax.shard_map(
        per_device,
        mesh=mesh,
        in_specs=(split,) * 4 + (held,) * 3,
        out_specs=(split,) * 3
        + (P(("node", "inner"), "rep", None),) * 2
        + (P(("node", "inner"), None, "rep"),),
        check_vma=False,
    )
```

```python
import functools

import jax
import jax.numpy as jnp
from jax import lax
from jax.experimental import pallas as pl
from jax.experimental.pallas import tpu as pltpu
from jax.sharding import PartitionSpec as P

BF16 = jnp.bfloat16
F32 = jnp.float32
LANES = 128
ROWS = 16
GROUP = 8
MESH = pl.DeviceIdType.MESH


def place(distance, nodes):
    if distance < nodes // 2:
        return GROUP * (distance // 4) + distance % 4
    back = nodes - 1 - distance
    return GROUP * (back // 4) + 4 + back % 4


def mm(a, b, contract):
    return lax.dot_general(a, b, ((contract[:1], contract[1:]), ((), ())), preferred_element_type=F32)


def kernel(
    sizes,
    tokens,
    out_grad,
    expert_ids,
    route_weight,
    gate_hbm,
    up_hbm,
    down_hbm,
    mixed,
    grad_tokens,
    grad_route,
    grad_gate,
    grad_up,
    grad_down,
    small,
    gathered,
    pick,
    slot_send,
    slot_got,
    answer_send,
    answer_got,
    partial,
    first,
    sums_left,
    sums_right,
    gate_w,
    up_w,
    down_w,
    terms,
    paired,
    crossed,
    weight_sem,
    ring_send,
    ring_recv,
    slot_send_sem,
    slot_recv_sem,
    answer_send_sem,
    answer_recv_sem,
    sum_send,
    sum_recv,
    pair_send,
    pair_recv,
    cross_send,
    cross_recv,
):
    nodes, inners, chips, width, ff, top, local = sizes
    chunks = nodes // GROUP
    half = nodes // 2
    total_lanes = 2 * width + LANES
    middle = (total_lanes // LANES + 1) // 2 * LANES
    halves = (pl.ds(0, middle), pl.ds(middle, total_lanes - middle))
    part = width // (2 * chips)
    node = lax.axis_index("node")
    inner = lax.axis_index("inner")
    rep = lax.axis_index("rep")
    chip = rep // 2
    core = lax.rem(rep, 2)
    right = {"node": lax.rem(node + 1, nodes)}
    left = {"node": lax.rem(node + nodes - 1, nodes)}
    partner = {"rep": rep + 1 - 2 * core}

    def inner_at(step):
        return {"inner": lax.rem(inner + step + inners, inners)}

    def chip_at(step):
        return {"rep": 2 * lax.rem(chip + step + chips, chips) + core}

    weight_copies = [
        pltpu.make_async_copy(src, dst, weight_sem.at[i])
        for i, (src, dst) in enumerate(((gate_hbm, gate_w), (up_hbm, up_w), (down_hbm, down_w)))
    ]
    for copy in weight_copies:
        copy.start()

    barrier = pltpu.get_barrier_semaphore()
    peers = (
        [right, left, partner]
        + [inner_at(d) for d in range(1, inners)]
        + [chip_at(d) for d in range(1, chips)]
    )
    for peer in peers:
        pl.semaphore_signal(barrier, inc=1, device_id=peer, device_id_type=MESH)

    small[...] = jnp.zeros_like(small)
    small[0, :, 0:top] = expert_ids[...].astype(F32)
    small[1, :, 0:top] = route_weight[...]
    weight = small[1]
    high = weight.astype(BF16).astype(F32)
    mid = (weight - high).astype(BF16).astype(F32)
    low = weight - high - mid
    meta = small[0] + pltpu.roll(high, 32, 1) + pltpu.roll(mid, 64, 1) + pltpu.roll(low, 96, 1)
    gathered[0:ROWS, 0:width] = tokens[...]
    gathered[0:ROWS, width : 2 * width] = out_grad[...]
    gathered[0:ROWS, 2 * width :] = meta.astype(BF16)

    pl.semaphore_wait(barrier, len(peers))
    pending = []

    def ring_copy(way, step, h):
        if way == 0:
            here, there, target = step, step + 1, right
        else:
            here, there, target = (nodes - step) % nodes, nodes - 1 - step, left
        return pltpu.make_async_remote_copy(
            src_ref=gathered.at[pl.ds(ROWS * place(here, nodes), ROWS), halves[h]],
            dst_ref=gathered.at[pl.ds(ROWS * place(there, nodes), ROWS), halves[h]],
            send_sem=ring_send.at[way, step, h],
            recv_sem=ring_recv.at[way, step, h],
            device_id=target,
            device_id_type=MESH,
        )

    steps = (half, half - 1)

    def ring_start(way, step, h):
        if step < steps[way]:
            copy = ring_copy(way, step, h)
            copy.start()
            pending.append(copy)

    def ring_wait(way, step, h):
        if step < steps[way]:
            ring_copy(way, step, h).wait_recv()

    per_chunk = inners * ROWS
    tokens_in = GROUP * ROWS

    def slot_copy(c, d):
        return pltpu.make_async_remote_copy(
            src_ref=slot_send.at[c, d],
            dst_ref=slot_got.at[c, d],
            send_sem=slot_send_sem.at[c, d],
            recv_sem=slot_recv_sem.at[c, d],
            device_id=inner_at(d),
            device_id_type=MESH,
        )

    def select(c):
        rows = pl.ds(tokens_in * c, tokens_in)
        ids = gathered[rows, 2 * width :].astype(F32).T[0:ROWS]
        top_row = lax.broadcasted_iota(jnp.int32, (ROWS, tokens_in), 0) < top
        owner = lax.broadcasted_iota(jnp.int32, (GROUP, tokens_in), 1) // ROWS
        same = owner == lax.broadcasted_iota(jnp.int32, (GROUP, tokens_in), 0)
        blocks = []
        for d in range(inners):
            for e in range(local):
                expert = (node * inners + lax.rem(inner + d, inners)) * local + e
                hit = jnp.where(jnp.logical_and(top_row, ids == expert.astype(F32)), 1.0, 0.0)
                hit = jnp.max(hit, axis=0, keepdims=True)
                blocks.append(jnp.where(same, jnp.broadcast_to(hit, same.shape), 0.0))
        onehot = jnp.concatenate(blocks, axis=0)
        pick[c] = onehot
        picked = mm(onehot.astype(BF16), gathered[rows, :], (1, 0)).astype(BF16)
        slot_got[c, 0] = picked[0:ROWS]
        for d in range(1, inners):
            slot_send[c, d] = picked[ROWS * d : ROWS * (d + 1)]
            copy = slot_copy(c, d)
            copy.start()
            pending.append(copy)

    for h in range(2):
        for way in range(2):
            ring_start(way, 0, h)
    for step in range(1, half + 1):
        for h in range(2):
            for way in range(2):
                ring_wait(way, step - 1, h)
                ring_start(way, step, h)
        if step % 4 == 0:
            select(step // 4 - 1)

    for copy in weight_copies:
        copy.wait()
    for c in range(chunks):
        for d in range(1, inners):
            slot_copy(c, d).wait_recv()

    count = nodes * inners
    blocks = chunks * inners
    lane = lax.broadcasted_iota(jnp.int32, (count, LANES), 1) < top

    def of_expert(lanes, e):
        rows = slot_got[:, :, :, lanes].astype(F32)
        return rows.reshape(blocks, local, GROUP, rows.shape[-1])[:, e].reshape(count, rows.shape[-1])

    results = []
    for e in range(local):
        rows = of_expert(slice(0, width), e).astype(BF16)
        cotangent = of_expert(slice(width, 2 * width), e)
        extra = of_expert(slice(2 * width, total_lanes), e)
        expert = (node * inners + inner) * local + e
        mine = jnp.logical_and(lane, extra == expert.astype(F32))
        weights = pltpu.roll(extra, 96, 1) + pltpu.roll(extra, 64, 1) + pltpu.roll(extra, 32, 1)
        weight = jnp.sum(jnp.where(mine, weights, 0.0), axis=1, keepdims=True)
        scaled = (weight * cotangent).astype(BF16)
        gate_pre = mm(rows, gate_w[e], (1, 0))
        up_pre = mm(rows, up_w[e], (1, 0))
        act_grad = mm(scaled, down_w[e], (1, 1))
        gate_sig = jax.nn.sigmoid(gate_pre)
        silu = gate_pre * gate_sig
        activation = (silu * up_pre).astype(BF16)
        up_grad = (act_grad * silu).astype(BF16)
        gate_grad = (act_grad * up_pre * (gate_sig * (1.0 + gate_pre * (1.0 - gate_sig)))).astype(BF16)
        expert_out = mm(activation, down_w[e], (1, 0))
        back = mm(gate_grad, gate_w[e], (1, 1)) + mm(up_grad, up_w[e], (1, 1))
        route = jnp.sum(cotangent * expert_out, axis=1, keepdims=True)
        route = jnp.where(mine, jnp.broadcast_to(route, mine.shape), 0.0)
        results.append((weight * expert_out, back, route, rows, scaled, activation, up_grad, gate_grad))

    for i, lanes in enumerate((slice(0, width), slice(width, 2 * width), slice(2 * width, total_lanes))):
        both = [results[e][i].reshape(blocks, 1, GROUP, -1) for e in range(local)]
        both = jnp.concatenate(both, axis=1).reshape(chunks, inners, ROWS, -1).astype(BF16)
        answer_send[:, :, :, lanes] = both
        answer_got[:, 0, :, lanes] = both[:, 0]

    def answer_copy(c, d):
        return pltpu.make_async_remote_copy(
            src_ref=answer_send.at[c, d],
            dst_ref=answer_got.at[c, d],
            send_sem=answer_send_sem.at[c, d],
            recv_sem=answer_recv_sem.at[c, d],
            device_id=inner_at(-d),
            device_id_type=MESH,
        )

    for c in reversed(range(chunks)):
        for d in range(1, inners):
            copy = answer_copy(c, d)
            copy.start()
            pending.append(copy)

    for e in range(local):
        _, _, _, rows, scaled, activation, up_grad, gate_grad = results[e]
        for i, grad in enumerate((gate_grad, up_grad)):
            term = mm(rows, grad, (0, 0)).astype(BF16)
            for r in range(2 * chips):
                at = (i * local + e) * part
                terms[r % 2, r // 2, at : at + part, :] = term[r * part : (r + 1) * part]
        term = mm(activation, scaled, (0, 0)).astype(BF16)
        for r in range(2 * chips):
            at = 2 * local * part
            terms[r % 2, r // 2, at : at + ff, e * part : (e + 1) * part] = term[:, r * part : (r + 1) * part]

    def pair_copy(d):
        return pltpu.make_async_remote_copy(
            src_ref=terms.at[1 - core, lax.rem(chip + d, chips)],
            dst_ref=paired.at[d],
            send_sem=pair_send.at[d],
            recv_sem=pair_recv.at[d],
            device_id=partner,
            device_id_type=MESH,
        )

    def cross_copy(d):
        return pltpu.make_async_remote_copy(
            src_ref=paired.at[d],
            dst_ref=crossed.at[d - 1],
            send_sem=cross_send.at[d - 1],
            recv_sem=cross_recv.at[d - 1],
            device_id=chip_at(d),
            device_id_type=MESH,
        )

    order = sorted(range(chips), key=lambda d: -min(d, chips - d))
    for d in order:
        copy = pair_copy(d)
        copy.start()
        pending.append(copy)

    def pair_add(d):
        pair_copy(d).wait_recv()
        own = terms[core, lax.rem(chip + d, chips)]
        paired[d] = (paired[d].astype(F32) + own.astype(F32)).astype(BF16)
        if d > 0:
            copy = cross_copy(d)
            copy.start()
            pending.append(copy)

    def combine(c):
        for d in range(1, inners):
            answer_copy(c, d).wait_recv()
        answers = answer_got[c].reshape(per_chunk, total_lanes)
        partial[pl.ds(tokens_in * c, tokens_in), :] = mm(pick[c].astype(BF16), answers, (0, 0))

    def partial_of(distance, h):
        return partial[pl.ds(ROWS * place(distance % nodes, nodes), ROWS), halves[h]]

    landed = (sums_left, sums_right)

    def sum_copy(way, step, h):
        source = first.at[way] if step == 0 else landed[way].at[step - 1]
        return pltpu.make_async_remote_copy(
            src_ref=source.at[:, halves[h]],
            dst_ref=landed[way].at[step, :, halves[h]],
            send_sem=sum_send.at[way, step, h],
            recv_sem=sum_recv.at[way, step, h],
            device_id=(left, right)[way],
            device_id_type=MESH,
        )

    def sum_step(way, step, h):
        distance = half - step if way == 0 else half + 1 + step
        mine = partial_of(distance, h)
        if step == 0:
            first[way, :, halves[h]] = mine.astype(BF16)
        else:
            sum_copy(way, step - 1, h).wait_recv()
            got = landed[way][step - 1, :, halves[h]]
            landed[way][step - 1, :, halves[h]] = (got.astype(F32) + mine).astype(BF16)
        copy = sum_copy(way, step, h)
        copy.start()
        pending.append(copy)

    combine(chunks - 1)
    beside = {}
    for k in range(1, chunks):
        beside.setdefault(4 * k - 3, []).append(functools.partial(combine, chunks - 1 - k))
    for k, d in enumerate(order):
        beside.setdefault(min(2 + k, half - 2), []).append(functools.partial(pair_add, d))
    for step in range(half):
        for h in range(2):
            for way in range(2):
                if step < steps[way]:
                    sum_step(way, step, h)
        for work in beside.get(step, ()):
            work()

    at = 0
    summed = paired[0].astype(F32)
    for d in range(1, chips):
        cross_copy(d).wait_recv()
        summed = summed + crossed[d - 1].astype(F32)
    summed = summed.astype(BF16)
    for i, out in enumerate((grad_gate, grad_up)):
        for e in range(local):
            at = (i * local + e) * part
            out[e] = summed[at : at + part]
    at = 2 * local * part
    for e in range(local):
        grad_down[e] = summed[at : at + ff, e * part : (e + 1) * part]

    for h in range(2):
        for way in range(2):
            sum_copy(way, steps[way] - 1, h).wait_recv()
    total = partial[0:ROWS, :] + sums_left[half - 1].astype(F32) + sums_right[half - 2].astype(F32)
    mixed[...] = total[:, 0:width].astype(BF16)
    grad_tokens[...] = total[:, width : 2 * width].astype(BF16)
    grad_route[...] = total[:, 2 * width :][:, 0:top]

    for copy in pending:
        copy.wait_send()


def per_device(tokens, out_grad, expert_ids, route_weight, gate_weight, up_weight, down_weight):
    width = tokens.shape[1]
    top = expert_ids.shape[1]
    local, _, ff = gate_weight.shape
    nodes = lax.axis_size("node")
    inners = lax.axis_size("inner")
    reps = lax.axis_size("rep")
    chips = reps // 2
    part = width // reps
    lanes = 2 * width + LANES
    chunks = nodes // GROUP
    half = nodes // 2
    slice_shape = (2 * local * part + ff, ff)
    count = nodes * ROWS
    vmem = pl.BlockSpec(memory_space=pltpu.VMEM)
    anywhere = pl.BlockSpec(memory_space=pl.ANY)
    dma = pltpu.SemaphoreType.DMA
    others = max(1, chips - 1)
    return pl.pallas_call(
        functools.partial(kernel, (nodes, inners, chips, width, ff, top, local)),
        out_shape=(
            jax.ShapeDtypeStruct((ROWS, width), BF16),
            jax.ShapeDtypeStruct((ROWS, width), BF16),
            jax.ShapeDtypeStruct((ROWS, top), F32),
            jax.ShapeDtypeStruct((local, part, ff), BF16),
            jax.ShapeDtypeStruct((local, part, ff), BF16),
            jax.ShapeDtypeStruct((local, ff, part), BF16),
        ),
        in_specs=[vmem] * 4 + [anywhere] * 3,
        out_specs=[vmem] * 6,
        scratch_shapes=[
            pltpu.VMEM((2, ROWS, LANES), F32),
            pltpu.VMEM((count, lanes), BF16),
            pltpu.VMEM((chunks, inners * ROWS, GROUP * ROWS), F32),
            pltpu.VMEM((chunks, inners, ROWS, lanes), BF16),
            pltpu.VMEM((chunks, inners, ROWS, lanes), BF16),
            pltpu.VMEM((chunks, inners, ROWS, lanes), BF16),
            pltpu.VMEM((chunks, inners, ROWS, lanes), BF16),
            pltpu.VMEM((count, lanes), F32),
            pltpu.VMEM((2, ROWS, lanes), BF16),
            pltpu.VMEM((half, ROWS, lanes), BF16),
            pltpu.VMEM((half - 1, ROWS, lanes), BF16),
            pltpu.VMEM(gate_weight.shape, BF16),
            pltpu.VMEM(up_weight.shape, BF16),
            pltpu.VMEM(down_weight.shape, BF16),
            pltpu.VMEM((2, chips) + slice_shape, BF16),
            pltpu.VMEM((chips,) + slice_shape, BF16),
            pltpu.VMEM((others,) + slice_shape, BF16),
            dma((3,)),
            dma((2, half, 2)),
            dma((2, half, 2)),
            dma((chunks, inners)),
            dma((chunks, inners)),
            dma((chunks, inners)),
            dma((chunks, inners)),
            dma((2, half, 2)),
            dma((2, half, 2)),
            dma((chips,)),
            dma((chips,)),
            dma((others,)),
            dma((others,)),
        ],
        compiler_params=pltpu.CompilerParams(
            collective_id=0, has_side_effects=True, vmem_limit_bytes=56 * 1024 * 1024
        ),
        cost_estimate=pl.CostEstimate(
            flops=2 * 9 * local * count // ROWS * inners * width * ff,
            bytes_accessed=12 * local * width * ff,
            transcendentals=local * count * ff,
        ),
    )(tokens, out_grad, expert_ids, route_weight, gate_weight, up_weight, down_weight)


def solution(mesh):
    split = P(("node", "inner", "rep"), None)
    held = P(("node", "inner"), None, None)
    return jax.shard_map(
        per_device,
        mesh=mesh,
        in_specs=(split,) * 4 + (held,) * 3,
        out_specs=(split,) * 3
        + (P(("node", "inner"), "rep", None),) * 2
        + (P(("node", "inner"), None, "rep"),),
        check_vma=False,
    )
```

```python
import functools

import jax
import jax.numpy as jnp
from jax import lax
from jax.experimental import pallas as pl
from jax.experimental.pallas import tpu as pltpu
from jax.sharding import PartitionSpec as P

BF16 = jnp.bfloat16
F32 = jnp.float32
LANES = 128
ROWS = 16
GROUP = 8
MESH = pl.DeviceIdType.MESH
OUT_STRIDE = 3
BACK_STRIDE = 3
ADD_FROM = 4
ADD_EVERY = 2
SPLIT = 2


def place(distance, nodes):
    if distance < nodes // 2:
        return GROUP * (distance // 4) + distance % 4
    back = nodes - 1 - distance
    return GROUP * (back // 4) + 4 + back % 4


def parent_of(distance, stride):
    return distance - stride if distance % stride == 0 else distance - 1


def tree_order(half, stride):
    when = {0: 0.0}
    after = {distance: [] for distance in range(half + 1)}
    for distance in range(1, half + 1):
        parent = parent_of(distance, stride)
        after[parent].insert(0, distance)
        when[distance] = when[parent] + 2.6 + 0.65 * (distance - parent)
    for followers in after.values():
        followers.sort(reverse=True)
    return sorted(when, key=lambda distance: when[distance]), after


def mm(a, b, contract):
    return lax.dot_general(a, b, ((contract[:1], contract[1:]), ((), ())), preferred_element_type=F32)


def kernel(
    sizes,
    tokens,
    out_grad,
    expert_ids,
    route_weight,
    gate_hbm,
    up_hbm,
    down_hbm,
    mixed,
    grad_tokens,
    grad_route,
    grad_gate,
    grad_up,
    grad_down,
    small,
    gathered,
    pick,
    slot_send,
    slot_got,
    answer_send,
    answer_got,
    partial,
    sums_out,
    sums_in,
    gate_w,
    up_w,
    down_w,
    terms,
    paired,
    crossed,
    weight_sem,
    ring_send,
    ring_recv,
    slot_send_sem,
    slot_recv_sem,
    answer_send_sem,
    answer_recv_sem,
    sum_send,
    sum_recv,
    pair_send,
    pair_recv,
    cross_send,
    cross_recv,
):
    nodes, inners, chips, width, ff, top, local = sizes
    chunks = nodes // GROUP
    half = nodes // 2
    total_lanes = 2 * width + LANES
    middle = (total_lanes // LANES + 1) // 2 * LANES
    halves = (pl.ds(0, middle), pl.ds(middle, total_lanes - middle))
    part = width // (2 * chips)
    node = lax.axis_index("node")
    inner = lax.axis_index("inner")
    rep = lax.axis_index("rep")
    chip = rep // 2
    core = lax.rem(rep, 2)
    partner = {"rep": rep + 1 - 2 * core}

    def node_at(step):
        return {"node": lax.rem(node + step + nodes, nodes)}

    def inner_at(step):
        return {"inner": lax.rem(inner + step + inners, inners)}

    def chip_at(step):
        return {"rep": 2 * lax.rem(chip + step + chips, chips) + core}

    weight_copies = [
        pltpu.make_async_copy(src, dst, weight_sem.at[i])
        for i, (src, dst) in enumerate(((gate_hbm, gate_w), (up_hbm, up_w), (down_hbm, down_w)))
    ]
    for copy in weight_copies:
        copy.start()

    barrier = pltpu.get_barrier_semaphore()
    peers = (
        [node_at(way * step) for step in sorted({1, OUT_STRIDE, BACK_STRIDE}) for way in (1, -1)]
        + [partner]
        + [inner_at(d) for d in range(1, inners)]
        + [chip_at(d) for d in range(1, chips)]
    )
    for peer in peers:
        pl.semaphore_signal(barrier, inc=1, device_id=peer, device_id_type=MESH)

    small[...] = jnp.zeros_like(small)
    small[0, :, 0:top] = expert_ids[...].astype(F32)
    small[1, :, 0:top] = route_weight[...]
    weight = small[1]
    high = weight.astype(BF16).astype(F32)
    mid = (weight - high).astype(BF16).astype(F32)
    low = weight - high - mid
    meta = small[0] + pltpu.roll(high, 32, 1) + pltpu.roll(mid, 64, 1) + pltpu.roll(low, 96, 1)
    gathered[0:ROWS, 0:width] = tokens[...]
    gathered[0:ROWS, width : 2 * width] = out_grad[...]
    gathered[0:ROWS, 2 * width :] = meta.astype(BF16)

    pl.semaphore_wait(barrier, len(peers))
    pending = []

    order, after = tree_order(half, OUT_STRIDE)
    back_order, back_after = tree_order(half, BACK_STRIDE)
    back_order = [distance for distance in reversed(back_order) if distance > 0]
    reach = (half, half - 1)

    def at(way, distance):
        return place(distance if way == 0 else (nodes - distance) % nodes, nodes)

    def block(way, distance):
        return pl.ds(ROWS * at(way, distance), ROWS)

    def gather_copy(way, distance, h):
        parent = parent_of(distance, OUT_STRIDE)
        return pltpu.make_async_remote_copy(
            src_ref=gathered.at[block(way, parent), halves[h]],
            dst_ref=gathered.at[block(way, distance), halves[h]],
            send_sem=ring_send.at[way, distance - 1, h],
            recv_sem=ring_recv.at[way, distance - 1, h],
            device_id=node_at((distance - parent) * (1, -1)[way]),
            device_id_type=MESH,
        )

    per_chunk = inners * ROWS
    tokens_in = GROUP * ROWS

    def slot_copy(c, d):
        return pltpu.make_async_remote_copy(
            src_ref=slot_send.at[c, d],
            dst_ref=slot_got.at[c, d],
            send_sem=slot_send_sem.at[c, d],
            recv_sem=slot_recv_sem.at[c, d],
            device_id=inner_at(d),
            device_id_type=MESH,
        )

    def select(c):
        rows = pl.ds(tokens_in * c, tokens_in)
        ids = gathered[rows, 2 * width :].astype(F32).T[0:ROWS]
        top_row = lax.broadcasted_iota(jnp.int32, (ROWS, tokens_in), 0) < top
        owner = lax.broadcasted_iota(jnp.int32, (GROUP, tokens_in), 1) // ROWS
        same = owner == lax.broadcasted_iota(jnp.int32, (GROUP, tokens_in), 0)
        blocks = []
        for d in range(inners):
            for e in range(local):
                expert = (node * inners + lax.rem(inner + d, inners)) * local + e
                hit = jnp.where(jnp.logical_and(top_row, ids == expert.astype(F32)), 1.0, 0.0)
                hit = jnp.max(hit, axis=0, keepdims=True)
                blocks.append(jnp.where(same, jnp.broadcast_to(hit, same.shape), 0.0))
        onehot = jnp.concatenate(blocks, axis=0)
        pick[c] = onehot
        picked = mm(onehot.astype(BF16), gathered[rows, :], (1, 0)).astype(BF16)
        slot_got[c, 0] = picked[0:ROWS]
        for d in range(1, inners):
            slot_send[c, d] = picked[ROWS * d : ROWS * (d + 1)]
            copy = slot_copy(c, d)
            copy.start()
            pending.append(copy)

    batches = [range(0, chunks // 2), range(chunks // 2, chunks)]
    if SPLIT == 3 and chunks == 4:
        batches = [range(0, 2), range(2, 3), range(3, 4)]
    kept = [[] for _ in range(local)]

    def of_expert(batch, lanes, e):
        rows = slot_got[batch.start : batch.stop, :, :, lanes].astype(F32)
        rows = rows.reshape(len(batch) * inners, local, GROUP, rows.shape[-1])[:, e]
        return rows.reshape(len(batch) * inners * GROUP, rows.shape[-1])

    def experts(batch):
        results = []
        for e in range(local):
            rows = of_expert(batch, slice(0, width), e).astype(BF16)
            cotangent = of_expert(batch, slice(width, 2 * width), e)
            extra = of_expert(batch, slice(2 * width, total_lanes), e)
            lane = lax.broadcasted_iota(jnp.int32, extra.shape, 1) < top
            expert = (node * inners + inner) * local + e
            mine = jnp.logical_and(lane, extra == expert.astype(F32))
            weights = pltpu.roll(extra, 96, 1) + pltpu.roll(extra, 64, 1) + pltpu.roll(extra, 32, 1)
            weight = jnp.sum(jnp.where(mine, weights, 0.0), axis=1, keepdims=True)
            scaled = (weight * cotangent).astype(BF16)
            gate_pre = mm(rows, gate_w[e], (1, 0))
            up_pre = mm(rows, up_w[e], (1, 0))
            yield
            act_grad = mm(scaled, down_w[e], (1, 1))
            gate_sig = jax.nn.sigmoid(gate_pre)
            silu = gate_pre * gate_sig
            activation = (silu * up_pre).astype(BF16)
            up_grad = (act_grad * silu).astype(BF16)
            gate_grad = act_grad * up_pre * (gate_sig * (1.0 + gate_pre * (1.0 - gate_sig)))
            gate_grad = gate_grad.astype(BF16)
            yield
            expert_out = mm(activation, down_w[e], (1, 0))
            back = mm(gate_grad, gate_w[e], (1, 1)) + mm(up_grad, up_w[e], (1, 1))
            route = jnp.sum(cotangent * expert_out, axis=1, keepdims=True)
            route = jnp.where(mine, jnp.broadcast_to(route, mine.shape), 0.0)
            results.append((weight * expert_out, back, route))
            kept[e].append((rows, scaled, activation, up_grad, gate_grad))
            yield
        for i, lanes in enumerate((slice(0, width), slice(width, 2 * width), slice(2 * width, total_lanes))):
            both = [results[e][i].reshape(len(batch) * inners, 1, GROUP, -1) for e in range(local)]
            both = jnp.concatenate(both, axis=1).reshape(len(batch), inners, ROWS, -1).astype(BF16)
            answer_send[batch.start : batch.stop, :, :, lanes] = both
            answer_got[batch.start : batch.stop, 0, :, lanes] = both[:, 0]

    def answer_copy(c, d):
        return pltpu.make_async_remote_copy(
            src_ref=answer_send.at[c, d],
            dst_ref=answer_got.at[c, d],
            send_sem=answer_send_sem.at[c, d],
            recv_sem=answer_recv_sem.at[c, d],
            device_id=inner_at(-d),
            device_id_type=MESH,
        )

    def serve(batch):
        for c in batch:
            for d in range(1, inners):
                slot_copy(c, d).wait_recv()
        yield from experts(batch)
        for c in reversed(batch):
            for d in range(1, inners):
                copy = answer_copy(c, d)
                copy.start()
                pending.append(copy)

    early = serve(batches[0])
    rest = None
    seen = set()
    for distance in order:
        for h in range(2):
            for way in range(2):
                if distance > reach[way]:
                    continue
                if distance > 0:
                    gather_copy(way, distance, h).wait_recv()
                for follower in after[distance]:
                    if follower <= reach[way]:
                        copy = gather_copy(way, follower, h)
                        copy.start()
                        pending.append(copy)
        before = set(seen)
        seen.update(at(way, distance) for way in range(2) if distance <= reach[way])
        if rest is not None:
            rest += 1
            if rest == 2:
                for copy in weight_copies:
                    copy.wait()
            if rest >= 2:
                next(early, None)
        for c in range(chunks):
            wanted = set(range(GROUP * c, GROUP * (c + 1)))
            if wanted <= seen and not wanted <= before:
                select(c)
                if c == batches[0][-1]:
                    rest = 0

    for batch in batches[1:]:
        for _ in early:
            pass
        early = serve(batch)
    for _ in early:
        pass

    for e in range(local):
        rows, scaled, activation, up_grad, gate_grad = (
            jnp.concatenate(pair, axis=0) for pair in zip(*kept[e])
        )
        for i, grad in enumerate((gate_grad, up_grad)):
            term = mm(rows, grad, (0, 0)).astype(BF16)
            for r in range(2 * chips):
                low = (i * local + e) * part
                terms[r % 2, r // 2, low : low + part, :] = term[r * part : (r + 1) * part]
        term = mm(activation, scaled, (0, 0)).astype(BF16)
        for r in range(2 * chips):
            low = 2 * local * part
            terms[r % 2, r // 2, low : low + ff, e * part : (e + 1) * part] = term[:, r * part : (r + 1) * part]

    def pair_copy(d):
        return pltpu.make_async_remote_copy(
            src_ref=terms.at[1 - core, lax.rem(chip + d, chips)],
            dst_ref=paired.at[d],
            send_sem=pair_send.at[d],
            recv_sem=pair_recv.at[d],
            device_id=partner,
            device_id_type=MESH,
        )

    def cross_copy(d):
        return pltpu.make_async_remote_copy(
            src_ref=paired.at[d],
            dst_ref=crossed.at[d - 1],
            send_sem=cross_send.at[d - 1],
            recv_sem=cross_recv.at[d - 1],
            device_id=chip_at(d),
            device_id_type=MESH,
        )

    chip_order = sorted(range(chips), key=lambda d: -min(d, chips - d))
    for d in chip_order:
        copy = pair_copy(d)
        copy.start()
        pending.append(copy)

    def pair_add(d):
        pair_copy(d).wait_recv()
        own = terms[core, lax.rem(chip + d, chips)]
        paired[d] = (paired[d].astype(F32) + own.astype(F32)).astype(BF16)
        if d > 0:
            copy = cross_copy(d)
            copy.start()
            pending.append(copy)

    def combine(c):
        for d in range(1, inners):
            answer_copy(c, d).wait_recv()
        answers = answer_got[c].reshape(per_chunk, total_lanes)
        partial[pl.ds(tokens_in * c, tokens_in), :] = mm(pick[c].astype(BF16), answers, (0, 0))

    def sum_copy(way, distance, h):
        parent = parent_of(distance, BACK_STRIDE)
        return pltpu.make_async_remote_copy(
            src_ref=sums_out.at[way, distance - 1, :, halves[h]],
            dst_ref=sums_in.at[way, distance - 1, :, halves[h]],
            send_sem=sum_send.at[way, distance - 1, h],
            recv_sem=sum_recv.at[way, distance - 1, h],
            device_id=node_at((distance - parent) * (-1, 1)[way]),
            device_id_type=MESH,
        )

    def arrived(way, distance, h):
        total = None
        for follower in back_after[distance]:
            if follower <= reach[way]:
                sum_copy(way, follower, h).wait_recv()
                got = sums_in[way, follower - 1, :, halves[h]].astype(F32)
                total = got if total is None else total + got
        return total

    combined = set()

    def combine_for(distance):
        for way in range(2):
            if 0 <= distance <= reach[way]:
                c = at(way, distance) // GROUP
                if c not in combined:
                    combined.add(c)
                    combine(c)

    add_every = ADD_EVERY if (chips - 1) * ADD_EVERY + ADD_FROM < half else 1
    first_add = ADD_FROM if add_every > 1 else 0
    combine_for(back_order[0])
    for step, distance in enumerate(back_order):
        combine_for(distance)
        for h in range(2):
            for way in range(2):
                if distance > reach[way]:
                    continue
                total = partial[block(way, distance), halves[h]]
                got = arrived(way, distance, h)
                if got is not None:
                    total = total + got
                sums_out[way, distance - 1, :, halves[h]] = total.astype(BF16)
                copy = sum_copy(way, distance, h)
                copy.start()
                pending.append(copy)
        for ahead in back_order[step + 1 : step + 3]:
            combine_for(ahead)
        turn, off = divmod(step - first_add, add_every)
        if off == 0 and 0 <= turn < chips:
            pair_add(chip_order[turn])
    for c in range(chunks):
        if c not in combined:
            combine(c)

    summed = paired[0].astype(F32)
    for d in range(1, chips):
        cross_copy(d).wait_recv()
        summed = summed + crossed[d - 1].astype(F32)
    summed = summed.astype(BF16)
    for i, out in enumerate((grad_gate, grad_up)):
        for e in range(local):
            low = (i * local + e) * part
            out[e] = summed[low : low + part]
    low = 2 * local * part
    for e in range(local):
        grad_down[e] = summed[low : low + ff, e * part : (e + 1) * part]

    for h, low in ((0, 0), (1, middle)):
        total = partial[0:ROWS, halves[h]] + arrived(0, 0, h) + arrived(1, 0, h)
        for out, begin, size in ((mixed, 0, width), (grad_tokens, width, width), (grad_route, 2 * width, LANES)):
            start, stop = max(begin, low), min(begin + size, low + total.shape[1])
            if start < stop:
                value = total[:, start - low : stop - low]
                if size == LANES:
                    out[...] = value[:, 0:top]
                else:
                    out[:, start - begin : stop - begin] = value.astype(BF16)

    for copy in pending:
        copy.wait_send()


def copy_out(*refs):
    count = (len(refs) - 1) // 2
    copies = [
        pltpu.make_async_copy(refs[i], refs[count + i], refs[-1].at[i]) for i in range(count)
    ]
    for copy in copies:
        copy.start()
    for copy in copies:
        copy.wait()


def per_device(tokens, out_grad, expert_ids, route_weight, gate_weight, up_weight, down_weight):
    width = tokens.shape[1]
    top = expert_ids.shape[1]
    local, _, ff = gate_weight.shape
    nodes = lax.axis_size("node")
    inners = lax.axis_size("inner")
    reps = lax.axis_size("rep")
    chips = reps // 2
    part = width // reps
    lanes = 2 * width + LANES
    chunks = nodes // GROUP
    half = nodes // 2
    slice_shape = (2 * local * part + ff, ff)
    count = nodes * ROWS
    vmem = pl.BlockSpec(memory_space=pltpu.VMEM)
    anywhere = pl.BlockSpec(memory_space=pl.ANY)
    dma = pltpu.SemaphoreType.DMA
    others = max(1, chips - 1)
    results = pl.pallas_call(
        functools.partial(kernel, (nodes, inners, chips, width, ff, top, local)),
        out_shape=(
            jax.ShapeDtypeStruct((ROWS, width), BF16),
            jax.ShapeDtypeStruct((ROWS, width), BF16),
            jax.ShapeDtypeStruct((ROWS, top), F32),
            jax.ShapeDtypeStruct((local, part, ff), BF16),
            jax.ShapeDtypeStruct((local, part, ff), BF16),
            jax.ShapeDtypeStruct((local, ff, part), BF16),
        ),
        in_specs=[vmem] * 4 + [anywhere] * 3,
        out_specs=[vmem] * 6,
        scratch_shapes=[
            pltpu.VMEM((2, ROWS, LANES), F32),
            pltpu.VMEM((count, lanes), BF16),
            pltpu.VMEM((chunks, inners * ROWS, GROUP * ROWS), F32),
            pltpu.VMEM((chunks, inners, ROWS, lanes), BF16),
            pltpu.VMEM((chunks, inners, ROWS, lanes), BF16),
            pltpu.VMEM((chunks, inners, ROWS, lanes), BF16),
            pltpu.VMEM((chunks, inners, ROWS, lanes), BF16),
            pltpu.VMEM((count, lanes), F32),
            pltpu.VMEM((2, half, ROWS, lanes), BF16),
            pltpu.VMEM((2, half, ROWS, lanes), BF16),
            pltpu.VMEM(gate_weight.shape, BF16),
            pltpu.VMEM(up_weight.shape, BF16),
            pltpu.VMEM(down_weight.shape, BF16),
            pltpu.VMEM((2, chips) + slice_shape, BF16),
            pltpu.VMEM((chips,) + slice_shape, BF16),
            pltpu.VMEM((others,) + slice_shape, BF16),
            dma((3,)),
            dma((2, half, 2)),
            dma((2, half, 2)),
            dma((chunks, inners)),
            dma((chunks, inners)),
            dma((chunks, inners)),
            dma((chunks, inners)),
            dma((2, half, 2)),
            dma((2, half, 2)),
            dma((chips,)),
            dma((chips,)),
            dma((others,)),
            dma((others,)),
        ],
        compiler_params=pltpu.CompilerParams(
            collective_id=0, has_side_effects=True, vmem_limit_bytes=56 * 1024 * 1024
        ),
        cost_estimate=pl.CostEstimate(
            flops=2 * 9 * local * count // ROWS * inners * width * ff,
            bytes_accessed=12 * local * width * ff,
            transcendentals=local * count * ff,
        ),
    )(tokens, out_grad, expert_ids, route_weight, gate_weight, up_weight, down_weight)
    return pl.pallas_call(
        copy_out,
        out_shape=[jax.ShapeDtypeStruct(result.shape, result.dtype) for result in results],
        in_specs=[anywhere] * len(results),
        out_specs=[anywhere] * len(results),
        scratch_shapes=[dma((len(results),))],
    )(*results)


def solution(mesh):
    split = P(("node", "inner", "rep"), None)
    held = P(("node", "inner"), None, None)
    return jax.shard_map(
        per_device,
        mesh=mesh,
        in_specs=(split,) * 4 + (held,) * 3,
        out_specs=(split,) * 3
        + (P(("node", "inner"), "rep", None),) * 2
        + (P(("node", "inner"), None, "rep"),),
        check_vma=False,
    )
```

```python
import functools

import jax
import jax.numpy as jnp
from jax import lax
from jax.experimental import pallas as pl
from jax.experimental.pallas import tpu as pltpu
from jax.sharding import PartitionSpec as P

BF16 = jnp.bfloat16
F32 = jnp.float32
LANES = 128
ROWS = 16
GROUP = 8
MESH = pl.DeviceIdType.MESH
OUT_STRIDE = 3
BACK_STRIDE = 3
ADD_FROM = 4
ADD_EVERY = 2


def place(distance, nodes):
    if distance < nodes // 2:
        return GROUP * (distance // 4) + distance % 4
    back = nodes - 1 - distance
    return GROUP * (back // 4) + 4 + back % 4


def parent_of(distance, stride):
    return distance - stride if distance % stride == 0 else distance - 1


def tree_order(half, stride):
    when = {0: 0.0}
    after = {distance: [] for distance in range(half + 1)}
    for distance in range(1, half + 1):
        parent = parent_of(distance, stride)
        after[parent].insert(0, distance)
        when[distance] = when[parent] + 2.6 + 0.65 * (distance - parent)
    for followers in after.values():
        followers.sort(reverse=True)
    return sorted(when, key=lambda distance: when[distance]), after


def mm(a, b, contract):
    return lax.dot_general(a, b, ((contract[:1], contract[1:]), ((), ())), preferred_element_type=F32)


def kernel(
    sizes,
    tokens,
    out_grad,
    expert_ids,
    route_weight,
    gate_hbm,
    up_hbm,
    down_hbm,
    mixed,
    grad_tokens,
    grad_route,
    grad_gate,
    grad_up,
    grad_down,
    small,
    gathered,
    pick,
    slot_send,
    slot_got,
    answer_send,
    answer_got,
    partial,
    sums_out,
    sums_in,
    gate_w,
    up_w,
    down_w,
    terms,
    paired,
    crossed,
    weight_sem,
    ring_send,
    ring_recv,
    slot_send_sem,
    slot_recv_sem,
    answer_send_sem,
    answer_recv_sem,
    sum_send,
    sum_recv,
    pair_send,
    pair_recv,
    cross_send,
    cross_recv,
):
    nodes, inners, chips, width, ff, top, local = sizes
    chunks = nodes // GROUP
    half = nodes // 2
    total_lanes = 2 * width + LANES
    middle = (total_lanes // LANES + 1) // 2 * LANES
    halves = (pl.ds(0, middle), pl.ds(middle, total_lanes - middle))
    part = width // (2 * chips)
    node = lax.axis_index("node")
    inner = lax.axis_index("inner")
    rep = lax.axis_index("rep")
    chip = rep // 2
    core = lax.rem(rep, 2)
    partner = {"rep": rep + 1 - 2 * core}

    def node_at(step):
        return {"node": lax.rem(node + step + nodes, nodes)}

    def inner_at(step):
        return {"inner": lax.rem(inner + step + inners, inners)}

    def chip_at(step):
        return {"rep": 2 * lax.rem(chip + step + chips, chips) + core}

    weight_copies = [
        pltpu.make_async_copy(src, dst, weight_sem.at[i])
        for i, (src, dst) in enumerate(((gate_hbm, gate_w), (up_hbm, up_w), (down_hbm, down_w)))
    ]
    for copy in weight_copies:
        copy.start()

    barrier = pltpu.get_barrier_semaphore()
    peers = (
        [node_at(way * step) for step in sorted({1, OUT_STRIDE, BACK_STRIDE}) for way in (1, -1)]
        + [partner]
        + [inner_at(d) for d in range(1, inners)]
        + [chip_at(d) for d in range(1, chips)]
    )
    for peer in peers:
        pl.semaphore_signal(barrier, inc=1, device_id=peer, device_id_type=MESH)

    small[...] = jnp.zeros_like(small)
    small[0, :, 0:top] = expert_ids[...].astype(F32)
    small[1, :, 0:top] = route_weight[...]
    weight = small[1]
    high = weight.astype(BF16).astype(F32)
    mid = (weight - high).astype(BF16).astype(F32)
    low = weight - high - mid
    meta = small[0] + pltpu.roll(high, 32, 1) + pltpu.roll(mid, 64, 1) + pltpu.roll(low, 96, 1)
    gathered[0:ROWS, 0:width] = tokens[...]
    gathered[0:ROWS, width : 2 * width] = out_grad[...]
    gathered[0:ROWS, 2 * width :] = meta.astype(BF16)

    pl.semaphore_wait(barrier, len(peers))
    pending = []

    order, after = tree_order(half, OUT_STRIDE)
    back_order, back_after = tree_order(half, BACK_STRIDE)
    back_order = [distance for distance in reversed(back_order) if distance > 0]
    reach = (half, half - 1)

    def at(way, distance):
        return place(distance if way == 0 else (nodes - distance) % nodes, nodes)

    def block(way, distance):
        return pl.ds(ROWS * at(way, distance), ROWS)

    def gather_copy(way, distance, h):
        parent = parent_of(distance, OUT_STRIDE)
        return pltpu.make_async_remote_copy(
            src_ref=gathered.at[block(way, parent), halves[h]],
            dst_ref=gathered.at[block(way, distance), halves[h]],
            send_sem=ring_send.at[way, distance - 1, h],
            recv_sem=ring_recv.at[way, distance - 1, h],
            device_id=node_at((distance - parent) * (1, -1)[way]),
            device_id_type=MESH,
        )

    per_chunk = inners * ROWS
    tokens_in = GROUP * ROWS

    def slot_copy(c, d):
        return pltpu.make_async_remote_copy(
            src_ref=slot_send.at[c, d],
            dst_ref=slot_got.at[c, d],
            send_sem=slot_send_sem.at[c, d],
            recv_sem=slot_recv_sem.at[c, d],
            device_id=inner_at(d),
            device_id_type=MESH,
        )

    def select(c):
        rows = pl.ds(tokens_in * c, tokens_in)
        ids = gathered[rows, 2 * width :].astype(F32).T[0:ROWS]
        top_row = lax.broadcasted_iota(jnp.int32, (ROWS, tokens_in), 0) < top
        owner = lax.broadcasted_iota(jnp.int32, (GROUP, tokens_in), 1) // ROWS
        same = owner == lax.broadcasted_iota(jnp.int32, (GROUP, tokens_in), 0)
        blocks = []
        for d in range(inners):
            for e in range(local):
                expert = (node * inners + lax.rem(inner + d, inners)) * local + e
                hit = jnp.where(jnp.logical_and(top_row, ids == expert.astype(F32)), 1.0, 0.0)
                hit = jnp.max(hit, axis=0, keepdims=True)
                blocks.append(jnp.where(same, jnp.broadcast_to(hit, same.shape), 0.0))
        onehot = jnp.concatenate(blocks, axis=0)
        pick[c] = onehot
        picked = mm(onehot.astype(BF16), gathered[rows, :], (1, 0)).astype(BF16)
        slot_got[c, 0] = picked[0:ROWS]
        for d in range(1, inners):
            slot_send[c, d] = picked[ROWS * d : ROWS * (d + 1)]
            copy = slot_copy(c, d)
            copy.start()
            pending.append(copy)

    batches = [range(0, chunks // 2), range(chunks // 2, chunks)]
    kept = [[] for _ in range(local)]

    def of_expert(batch, lanes, e):
        rows = slot_got[batch.start : batch.stop, :, :, lanes].astype(F32)
        rows = rows.reshape(len(batch) * inners, local, GROUP, rows.shape[-1])[:, e]
        return rows.reshape(len(batch) * inners * GROUP, rows.shape[-1])

    def experts(batch):
        results = []
        for e in range(local):
            rows = of_expert(batch, slice(0, width), e).astype(BF16)
            cotangent = of_expert(batch, slice(width, 2 * width), e)
            extra = of_expert(batch, slice(2 * width, total_lanes), e)
            lane = lax.broadcasted_iota(jnp.int32, extra.shape, 1) < top
            expert = (node * inners + inner) * local + e
            mine = jnp.logical_and(lane, extra == expert.astype(F32))
            weights = pltpu.roll(extra, 96, 1) + pltpu.roll(extra, 64, 1) + pltpu.roll(extra, 32, 1)
            weight = jnp.sum(jnp.where(mine, weights, 0.0), axis=1, keepdims=True)
            scaled = (weight * cotangent).astype(BF16)
            gate_pre = mm(rows, gate_w[e], (1, 0))
            up_pre = mm(rows, up_w[e], (1, 0))
            yield
            act_grad = mm(scaled, down_w[e], (1, 1))
            gate_sig = jax.nn.sigmoid(gate_pre)
            silu = gate_pre * gate_sig
            activation = (silu * up_pre).astype(BF16)
            up_grad = (act_grad * silu).astype(BF16)
            gate_grad = act_grad * up_pre * (gate_sig * (1.0 + gate_pre * (1.0 - gate_sig)))
            gate_grad = gate_grad.astype(BF16)
            yield
            expert_out = mm(activation, down_w[e], (1, 0))
            back = mm(gate_grad, gate_w[e], (1, 1)) + mm(up_grad, up_w[e], (1, 1))
            route = jnp.sum(cotangent * expert_out, axis=1, keepdims=True)
            route = jnp.where(mine, jnp.broadcast_to(route, mine.shape), 0.0)
            results.append((weight * expert_out, back, route))
            kept[e].append((rows, scaled, activation, up_grad, gate_grad))
            yield
        for i, lanes in enumerate((slice(0, width), slice(width, 2 * width), slice(2 * width, total_lanes))):
            both = [results[e][i].reshape(len(batch) * inners, 1, GROUP, -1) for e in range(local)]
            both = jnp.concatenate(both, axis=1).reshape(len(batch), inners, ROWS, -1).astype(BF16)
            answer_send[batch.start : batch.stop, :, :, lanes] = both
            answer_got[batch.start : batch.stop, 0, :, lanes] = both[:, 0]

    def answer_copy(c, d):
        return pltpu.make_async_remote_copy(
            src_ref=answer_send.at[c, d],
            dst_ref=answer_got.at[c, d],
            send_sem=answer_send_sem.at[c, d],
            recv_sem=answer_recv_sem.at[c, d],
            device_id=inner_at(-d),
            device_id_type=MESH,
        )

    def serve(batch):
        for c in batch:
            for d in range(1, inners):
                slot_copy(c, d).wait_recv()
        yield from experts(batch)
        for c in reversed(batch):
            for d in range(1, inners):
                copy = answer_copy(c, d)
                copy.start()
                pending.append(copy)

    early = serve(batches[0])
    rest = None
    seen = set()
    for distance in order:
        for h in range(2):
            for way in range(2):
                if distance > reach[way]:
                    continue
                if distance > 0:
                    gather_copy(way, distance, h).wait_recv()
                for follower in after[distance]:
                    if follower <= reach[way]:
                        copy = gather_copy(way, follower, h)
                        copy.start()
                        pending.append(copy)
        before = set(seen)
        seen.update(at(way, distance) for way in range(2) if distance <= reach[way])
        if rest is not None:
            rest += 1
            if rest == 2:
                for copy in weight_copies:
                    copy.wait()
            if rest >= 2:
                next(early, None)
        for c in range(chunks):
            wanted = set(range(GROUP * c, GROUP * (c + 1)))
            if wanted <= seen and not wanted <= before:
                select(c)
                if c == batches[0][-1]:
                    rest = 0

    for batch in batches[1:]:
        for _ in early:
            pass
        early = serve(batch)
    for _ in early:
        pass

    for e in range(local):
        rows, scaled, activation, up_grad, gate_grad = (
            jnp.concatenate(pair, axis=0) for pair in zip(*kept[e])
        )
        for i, grad in enumerate((gate_grad, up_grad)):
            term = mm(rows, grad, (0, 0)).astype(BF16)
            for r in range(2 * chips):
                low = (i * local + e) * part
                terms[r % 2, r // 2, low : low + part, :] = term[r * part : (r + 1) * part]
        term = mm(activation, scaled, (0, 0)).astype(BF16)
        for r in range(2 * chips):
            low = 2 * local * part
            terms[r % 2, r // 2, low : low + ff, e * part : (e + 1) * part] = term[:, r * part : (r + 1) * part]

    def pair_copy(d):
        return pltpu.make_async_remote_copy(
            src_ref=terms.at[1 - core, lax.rem(chip + d, chips)],
            dst_ref=paired.at[d],
            send_sem=pair_send.at[d],
            recv_sem=pair_recv.at[d],
            device_id=partner,
            device_id_type=MESH,
        )

    def cross_copy(d):
        return pltpu.make_async_remote_copy(
            src_ref=paired.at[d],
            dst_ref=crossed.at[d - 1],
            send_sem=cross_send.at[d - 1],
            recv_sem=cross_recv.at[d - 1],
            device_id=chip_at(d),
            device_id_type=MESH,
        )

    chip_order = sorted(range(chips), key=lambda d: -min(d, chips - d))
    for d in chip_order:
        copy = pair_copy(d)
        copy.start()
        pending.append(copy)

    def pair_add(d):
        pair_copy(d).wait_recv()
        own = terms[core, lax.rem(chip + d, chips)]
        paired[d] = (paired[d].astype(F32) + own.astype(F32)).astype(BF16)
        if d > 0:
            copy = cross_copy(d)
            copy.start()
            pending.append(copy)

    def combine(c):
        for d in range(1, inners):
            answer_copy(c, d).wait_recv()
        answers = answer_got[c].reshape(per_chunk, total_lanes)
        partial[pl.ds(tokens_in * c, tokens_in), :] = mm(pick[c].astype(BF16), answers, (0, 0))

    def sum_copy(way, distance, h):
        parent = parent_of(distance, BACK_STRIDE)
        return pltpu.make_async_remote_copy(
            src_ref=sums_out.at[way, distance - 1, :, halves[h]],
            dst_ref=sums_in.at[way, distance - 1, :, halves[h]],
            send_sem=sum_send.at[way, distance - 1, h],
            recv_sem=sum_recv.at[way, distance - 1, h],
            device_id=node_at((distance - parent) * (-1, 1)[way]),
            device_id_type=MESH,
        )

    def arrived(way, distance, h):
        total = None
        for follower in back_after[distance]:
            if follower <= reach[way]:
                sum_copy(way, follower, h).wait_recv()
                got = sums_in[way, follower - 1, :, halves[h]].astype(F32)
                total = got if total is None else total + got
        return total

    combined = set()

    def combine_for(distance):
        for way in range(2):
            if 0 <= distance <= reach[way]:
                c = at(way, distance) // GROUP
                if c not in combined:
                    combined.add(c)
                    combine(c)

    add_every = ADD_EVERY if (chips - 1) * ADD_EVERY + ADD_FROM < half else 1
    first_add = ADD_FROM if add_every > 1 else 0
    combine_for(back_order[0])
    for step, distance in enumerate(back_order):
        combine_for(distance)
        for h in range(2):
            for way in range(2):
                if distance > reach[way]:
                    continue
                total = partial[block(way, distance), halves[h]]
                got = arrived(way, distance, h)
                if got is not None:
                    total = total + got
                sums_out[way, distance - 1, :, halves[h]] = total.astype(BF16)
                copy = sum_copy(way, distance, h)
                copy.start()
                pending.append(copy)
        for ahead in back_order[step + 1 : step + 3]:
            combine_for(ahead)
        turn, off = divmod(step - first_add, add_every)
        if off == 0 and 0 <= turn < chips:
            pair_add(chip_order[turn])
    for c in range(chunks):
        if c not in combined:
            combine(c)

    summed = paired[0].astype(F32)
    for d in range(1, chips):
        cross_copy(d).wait_recv()
        summed = summed + crossed[d - 1].astype(F32)
    summed = summed.astype(BF16)
    for i, out in enumerate((grad_gate, grad_up)):
        for e in range(local):
            low = (i * local + e) * part
            out[e] = summed[low : low + part]
    low = 2 * local * part
    for e in range(local):
        grad_down[e] = summed[low : low + ff, e * part : (e + 1) * part]

    for h, low in ((0, 0), (1, middle)):
        total = partial[0:ROWS, halves[h]] + arrived(0, 0, h) + arrived(1, 0, h)
        for out, begin, size in ((mixed, 0, width), (grad_tokens, width, width), (grad_route, 2 * width, LANES)):
            start, stop = max(begin, low), min(begin + size, low + total.shape[1])
            if start < stop:
                value = total[:, start - low : stop - low]
                if size == LANES:
                    out[...] = value[:, 0:top]
                else:
                    out[:, start - begin : stop - begin] = value.astype(BF16)

    for copy in pending:
        copy.wait_send()


def copy_out(*refs):
    count = len(refs) // 2
    for source, target in zip(refs[:count], refs[count:]):
        target[...] = source[...]


def per_device(tokens, out_grad, expert_ids, route_weight, gate_weight, up_weight, down_weight):
    width = tokens.shape[1]
    top = expert_ids.shape[1]
    local, _, ff = gate_weight.shape
    nodes = lax.axis_size("node")
    inners = lax.axis_size("inner")
    reps = lax.axis_size("rep")
    chips = reps // 2
    part = width // reps
    lanes = 2 * width + LANES
    chunks = nodes // GROUP
    half = nodes // 2
    slice_shape = (2 * local * part + ff, ff)
    count = nodes * ROWS
    vmem = pl.BlockSpec(memory_space=pltpu.VMEM)
    anywhere = pl.BlockSpec(memory_space=pl.ANY)
    dma = pltpu.SemaphoreType.DMA
    others = max(1, chips - 1)
    results = pl.pallas_call(
        functools.partial(kernel, (nodes, inners, chips, width, ff, top, local)),
        out_shape=(
            jax.ShapeDtypeStruct((ROWS, width), BF16),
            jax.ShapeDtypeStruct((ROWS, width), BF16),
            jax.ShapeDtypeStruct((ROWS, top), F32),
            jax.ShapeDtypeStruct((local, part, ff), BF16),
            jax.ShapeDtypeStruct((local, part, ff), BF16),
            jax.ShapeDtypeStruct((local, ff, part), BF16),
        ),
        in_specs=[vmem] * 4 + [anywhere] * 3,
        out_specs=[vmem] * 6,
        scratch_shapes=[
            pltpu.VMEM((2, ROWS, LANES), F32),
            pltpu.VMEM((count, lanes), BF16),
            pltpu.VMEM((chunks, inners * ROWS, GROUP * ROWS), F32),
            pltpu.VMEM((chunks, inners, ROWS, lanes), BF16),
            pltpu.VMEM((chunks, inners, ROWS, lanes), BF16),
            pltpu.VMEM((chunks, inners, ROWS, lanes), BF16),
            pltpu.VMEM((chunks, inners, ROWS, lanes), BF16),
            pltpu.VMEM((count, lanes), F32),
            pltpu.VMEM((2, half, ROWS, lanes), BF16),
            pltpu.VMEM((2, half, ROWS, lanes), BF16),
            pltpu.VMEM(gate_weight.shape, BF16),
            pltpu.VMEM(up_weight.shape, BF16),
            pltpu.VMEM(down_weight.shape, BF16),
            pltpu.VMEM((2, chips) + slice_shape, BF16),
            pltpu.VMEM((chips,) + slice_shape, BF16),
            pltpu.VMEM((others,) + slice_shape, BF16),
            dma((3,)),
            dma((2, half, 2)),
            dma((2, half, 2)),
            dma((chunks, inners)),
            dma((chunks, inners)),
            dma((chunks, inners)),
            dma((chunks, inners)),
            dma((2, half, 2)),
            dma((2, half, 2)),
            dma((chips,)),
            dma((chips,)),
            dma((others,)),
            dma((others,)),
        ],
        compiler_params=pltpu.CompilerParams(
            collective_id=0, has_side_effects=True, vmem_limit_bytes=56 * 1024 * 1024
        ),
        cost_estimate=pl.CostEstimate(
            flops=2 * 9 * local * count // ROWS * inners * width * ff,
            bytes_accessed=12 * local * width * ff,
            transcendentals=local * count * ff,
        ),
    )(tokens, out_grad, expert_ids, route_weight, gate_weight, up_weight, down_weight)
    shapes = [jax.ShapeDtypeStruct(result.shape, result.dtype) for result in results]
    return pl.pallas_call(
        copy_out, out_shape=shapes, in_specs=[vmem] * len(results), out_specs=[vmem] * len(results)
    )(*results)


def solution(mesh):
    split = P(("node", "inner", "rep"), None)
    held = P(("node", "inner"), None, None)
    return jax.shard_map(
        per_device,
        mesh=mesh,
        in_specs=(split,) * 4 + (held,) * 3,
        out_specs=(split,) * 3
        + (P(("node", "inner"), "rep", None),) * 2
        + (P(("node", "inner"), None, "rep"),),
        check_vma=False,
    )
```

```python
import functools

import jax
import jax.numpy as jnp
from jax import lax
from jax.experimental import pallas as pl
from jax.experimental.pallas import tpu as pltpu
from jax.sharding import PartitionSpec as P

BF16 = jnp.bfloat16
F32 = jnp.float32
LANES = 128
ROWS = 16
GROUP = 8
MESH = pl.DeviceIdType.MESH
OUT_STRIDE = 3
BACK_STRIDE = 3
ADD_FROM = 4
ADD_EVERY = 2


def place(distance, nodes):
    if distance < nodes // 2:
        return GROUP * (distance // 4) + distance % 4
    back = nodes - 1 - distance
    return GROUP * (back // 4) + 4 + back % 4


def parent_of(distance, stride):
    return distance - stride if distance % stride == 0 else distance - 1


def tree_order(half, stride):
    when = {0: 0.0}
    after = {distance: [] for distance in range(half + 1)}
    for distance in range(1, half + 1):
        parent = parent_of(distance, stride)
        after[parent].insert(0, distance)
        when[distance] = when[parent] + 2.6 + 0.65 * (distance - parent)
    for followers in after.values():
        followers.sort(reverse=True)
    return sorted(when, key=lambda distance: when[distance]), after


def mm(a, b, contract):
    return lax.dot_general(a, b, ((contract[:1], contract[1:]), ((), ())), preferred_element_type=F32)


def kernel(
    sizes,
    tokens,
    out_grad,
    expert_ids,
    route_weight,
    gate_hbm,
    up_hbm,
    down_hbm,
    mixed,
    grad_tokens,
    grad_route,
    grad_gate,
    grad_up,
    grad_down,
    small,
    gathered,
    pick,
    slot_send,
    slot_got,
    answer_send,
    answer_got,
    partial,
    sums_out,
    sums_in,
    gate_w,
    up_w,
    down_w,
    terms,
    paired,
    crossed,
    weight_sem,
    ring_send,
    ring_recv,
    slot_send_sem,
    slot_recv_sem,
    answer_send_sem,
    answer_recv_sem,
    sum_send,
    sum_recv,
    pair_send,
    pair_recv,
    cross_send,
    cross_recv,
):
    nodes, inners, chips, width, ff, top, local = sizes
    chunks = nodes // GROUP
    half = nodes // 2
    total_lanes = 2 * width + LANES
    middle = (total_lanes // LANES + 1) // 2 * LANES
    halves = (pl.ds(0, middle), pl.ds(middle, total_lanes - middle))
    part = width // (2 * chips)
    node = lax.axis_index("node")
    inner = lax.axis_index("inner")
    rep = lax.axis_index("rep")
    chip = rep // 2
    core = lax.rem(rep, 2)
    partner = {"rep": rep + 1 - 2 * core}

    def node_at(step):
        return {"node": lax.rem(node + step + nodes, nodes)}

    def inner_at(step):
        return {"inner": lax.rem(inner + step + inners, inners)}

    def chip_at(step):
        return {"rep": 2 * lax.rem(chip + step + chips, chips) + core}

    weight_copies = [
        pltpu.make_async_copy(src, dst, weight_sem.at[i])
        for i, (src, dst) in enumerate(((gate_hbm, gate_w), (up_hbm, up_w), (down_hbm, down_w)))
    ]
    for copy in weight_copies:
        copy.start()

    barrier = pltpu.get_barrier_semaphore()
    peers = (
        [node_at(way * step) for step in sorted({1, OUT_STRIDE, BACK_STRIDE}) for way in (1, -1)]
        + [partner]
        + [inner_at(d) for d in range(1, inners)]
        + [chip_at(d) for d in range(1, chips)]
    )
    for peer in peers:
        pl.semaphore_signal(barrier, inc=1, device_id=peer, device_id_type=MESH)

    small[...] = jnp.zeros_like(small)
    small[0, :, 0:top] = expert_ids[...].astype(F32)
    small[1, :, 0:top] = route_weight[...]
    weight = small[1]
    high = weight.astype(BF16).astype(F32)
    mid = (weight - high).astype(BF16).astype(F32)
    low = weight - high - mid
    meta = small[0] + pltpu.roll(high, 32, 1) + pltpu.roll(mid, 64, 1) + pltpu.roll(low, 96, 1)
    gathered[0:ROWS, 0:width] = tokens[...]
    gathered[0:ROWS, width : 2 * width] = out_grad[...]
    gathered[0:ROWS, 2 * width :] = meta.astype(BF16)

    pl.semaphore_wait(barrier, len(peers))
    pending = []

    order, after = tree_order(half, OUT_STRIDE)
    back_order, back_after = tree_order(half, BACK_STRIDE)
    back_order = [distance for distance in reversed(back_order) if distance > 0]
    reach = (half, half - 1)

    def at(way, distance):
        return place(distance if way == 0 else (nodes - distance) % nodes, nodes)

    def block(way, distance):
        return pl.ds(ROWS * at(way, distance), ROWS)

    def gather_copy(way, distance, h):
        parent = parent_of(distance, OUT_STRIDE)
        return pltpu.make_async_remote_copy(
            src_ref=gathered.at[block(way, parent), halves[h]],
            dst_ref=gathered.at[block(way, distance), halves[h]],
            send_sem=ring_send.at[way, distance - 1, h],
            recv_sem=ring_recv.at[way, distance - 1, h],
            device_id=node_at((distance - parent) * (1, -1)[way]),
            device_id_type=MESH,
        )

    per_chunk = inners * ROWS
    tokens_in = GROUP * ROWS

    def slot_copy(c, d):
        return pltpu.make_async_remote_copy(
            src_ref=slot_send.at[c, d],
            dst_ref=slot_got.at[c, d],
            send_sem=slot_send_sem.at[c, d],
            recv_sem=slot_recv_sem.at[c, d],
            device_id=inner_at(d),
            device_id_type=MESH,
        )

    def select(c):
        rows = pl.ds(tokens_in * c, tokens_in)
        ids = gathered[rows, 2 * width :].astype(F32).T[0:ROWS]
        top_row = lax.broadcasted_iota(jnp.int32, (ROWS, tokens_in), 0) < top
        owner = lax.broadcasted_iota(jnp.int32, (GROUP, tokens_in), 1) // ROWS
        same = owner == lax.broadcasted_iota(jnp.int32, (GROUP, tokens_in), 0)
        blocks = []
        for d in range(inners):
            for e in range(local):
                expert = (node * inners + lax.rem(inner + d, inners)) * local + e
                hit = jnp.where(jnp.logical_and(top_row, ids == expert.astype(F32)), 1.0, 0.0)
                hit = jnp.max(hit, axis=0, keepdims=True)
                blocks.append(jnp.where(same, jnp.broadcast_to(hit, same.shape), 0.0))
        onehot = jnp.concatenate(blocks, axis=0)
        pick[c] = onehot
        picked = mm(onehot.astype(BF16), gathered[rows, :], (1, 0)).astype(BF16)
        slot_got[c, 0] = picked[0:ROWS]
        for d in range(1, inners):
            slot_send[c, d] = picked[ROWS * d : ROWS * (d + 1)]
            copy = slot_copy(c, d)
            copy.start()
            pending.append(copy)

    batches = [range(0, chunks - 1), range(chunks - 1, chunks)]
    kept = [[] for _ in range(local)]

    def of_expert(batch, lanes, e):
        rows = slot_got[batch.start : batch.stop, :, :, lanes].astype(F32)
        rows = rows.reshape(len(batch) * inners, local, GROUP, rows.shape[-1])[:, e]
        return rows.reshape(len(batch) * inners * GROUP, rows.shape[-1])

    def experts(batch):
        results = []
        for e in range(local):
            rows = of_expert(batch, slice(0, width), e).astype(BF16)
            cotangent = of_expert(batch, slice(width, 2 * width), e)
            extra = of_expert(batch, slice(2 * width, total_lanes), e)
            lane = lax.broadcasted_iota(jnp.int32, extra.shape, 1) < top
            expert = (node * inners + inner) * local + e
            mine = jnp.logical_and(lane, extra == expert.astype(F32))
            weights = pltpu.roll(extra, 96, 1) + pltpu.roll(extra, 64, 1) + pltpu.roll(extra, 32, 1)
            weight = jnp.sum(jnp.where(mine, weights, 0.0), axis=1, keepdims=True)
            scaled = (weight * cotangent).astype(BF16)
            gate_pre = mm(rows, gate_w[e], (1, 0))
            up_pre = mm(rows, up_w[e], (1, 0))
            yield
            act_grad = mm(scaled, down_w[e], (1, 1))
            gate_sig = jax.nn.sigmoid(gate_pre)
            silu = gate_pre * gate_sig
            activation = (silu * up_pre).astype(BF16)
            up_grad = (act_grad * silu).astype(BF16)
            gate_grad = act_grad * up_pre * (gate_sig * (1.0 + gate_pre * (1.0 - gate_sig)))
            gate_grad = gate_grad.astype(BF16)
            yield
            expert_out = mm(activation, down_w[e], (1, 0))
            back = mm(gate_grad, gate_w[e], (1, 1)) + mm(up_grad, up_w[e], (1, 1))
            route = jnp.sum(cotangent * expert_out, axis=1, keepdims=True)
            route = jnp.where(mine, jnp.broadcast_to(route, mine.shape), 0.0)
            results.append((weight * expert_out, back, route))
            kept[e].append((rows, scaled, activation, up_grad, gate_grad))
            yield
        for i, lanes in enumerate((slice(0, width), slice(width, 2 * width), slice(2 * width, total_lanes))):
            both = [results[e][i].reshape(len(batch) * inners, 1, GROUP, -1) for e in range(local)]
            both = jnp.concatenate(both, axis=1).reshape(len(batch), inners, ROWS, -1).astype(BF16)
            answer_send[batch.start : batch.stop, :, :, lanes] = both
            answer_got[batch.start : batch.stop, 0, :, lanes] = both[:, 0]

    def answer_copy(c, d):
        return pltpu.make_async_remote_copy(
            src_ref=answer_send.at[c, d],
            dst_ref=answer_got.at[c, d],
            send_sem=answer_send_sem.at[c, d],
            recv_sem=answer_recv_sem.at[c, d],
            device_id=inner_at(-d),
            device_id_type=MESH,
        )

    def serve(batch):
        for c in batch:
            for d in range(1, inners):
                slot_copy(c, d).wait_recv()
        yield from experts(batch)
        for c in reversed(batch):
            for d in range(1, inners):
                copy = answer_copy(c, d)
                copy.start()
                pending.append(copy)

    early = serve(batches[0])
    rest = None
    seen = set()
    for distance in order:
        for h in range(2):
            for way in range(2):
                if distance > reach[way]:
                    continue
                if distance > 0:
                    gather_copy(way, distance, h).wait_recv()
                for follower in after[distance]:
                    if follower <= reach[way]:
                        copy = gather_copy(way, follower, h)
                        copy.start()
                        pending.append(copy)
        before = set(seen)
        seen.update(at(way, distance) for way in range(2) if distance <= reach[way])
        if rest is not None:
            rest += 1
            if rest == 2:
                for copy in weight_copies:
                    copy.wait()
            if rest >= 2:
                next(early, None)
        for c in range(chunks):
            wanted = set(range(GROUP * c, GROUP * (c + 1)))
            if wanted <= seen and not wanted <= before:
                select(c)
                if c == batches[0][-1]:
                    rest = 0

    for batch in batches[1:]:
        for _ in early:
            pass
        early = serve(batch)
    for _ in early:
        pass

    for e in range(local):
        rows, scaled, activation, up_grad, gate_grad = (
            jnp.concatenate(pair, axis=0) for pair in zip(*kept[e])
        )
        for i, grad in enumerate((gate_grad, up_grad)):
            term = mm(rows, grad, (0, 0)).astype(BF16)
            for r in range(2 * chips):
                low = (i * local + e) * part
                terms[r % 2, r // 2, low : low + part, :] = term[r * part : (r + 1) * part]
        term = mm(activation, scaled, (0, 0)).astype(BF16)
        for r in range(2 * chips):
            low = 2 * local * part
            terms[r % 2, r // 2, low : low + ff, e * part : (e + 1) * part] = term[:, r * part : (r + 1) * part]

    def pair_copy(d):
        return pltpu.make_async_remote_copy(
            src_ref=terms.at[1 - core, lax.rem(chip + d, chips)],
            dst_ref=paired.at[d],
            send_sem=pair_send.at[d],
            recv_sem=pair_recv.at[d],
            device_id=partner,
            device_id_type=MESH,
        )

    def cross_copy(d):
        return pltpu.make_async_remote_copy(
            src_ref=paired.at[d],
            dst_ref=crossed.at[d - 1],
            send_sem=cross_send.at[d - 1],
            recv_sem=cross_recv.at[d - 1],
            device_id=chip_at(d),
            device_id_type=MESH,
        )

    chip_order = sorted(range(chips), key=lambda d: -min(d, chips - d))
    for d in chip_order:
        copy = pair_copy(d)
        copy.start()
        pending.append(copy)

    def pair_add(d):
        pair_copy(d).wait_recv()
        own = terms[core, lax.rem(chip + d, chips)]
        paired[d] = (paired[d].astype(F32) + own.astype(F32)).astype(BF16)
        if d > 0:
            copy = cross_copy(d)
            copy.start()
            pending.append(copy)

    def combine(c):
        for d in range(1, inners):
            answer_copy(c, d).wait_recv()
        answers = answer_got[c].reshape(per_chunk, total_lanes)
        partial[pl.ds(tokens_in * c, tokens_in), :] = mm(pick[c].astype(BF16), answers, (0, 0))

    def sum_copy(way, distance, h):
        parent = parent_of(distance, BACK_STRIDE)
        return pltpu.make_async_remote_copy(
            src_ref=sums_out.at[way, distance - 1, :, halves[h]],
            dst_ref=sums_in.at[way, distance - 1, :, halves[h]],
            send_sem=sum_send.at[way, distance - 1, h],
            recv_sem=sum_recv.at[way, distance - 1, h],
            device_id=node_at((distance - parent) * (-1, 1)[way]),
            device_id_type=MESH,
        )

    def arrived(way, distance, h):
        total = None
        for follower in back_after[distance]:
            if follower <= reach[way]:
                sum_copy(way, follower, h).wait_recv()
                got = sums_in[way, follower - 1, :, halves[h]].astype(F32)
                total = got if total is None else total + got
        return total

    combined = set()

    def combine_for(distance):
        for way in range(2):
            if 0 <= distance <= reach[way]:
                c = at(way, distance) // GROUP
                if c not in combined:
                    combined.add(c)
                    combine(c)

    add_every = ADD_EVERY if (chips - 1) * ADD_EVERY + ADD_FROM < half else 1
    first_add = ADD_FROM if add_every > 1 else 0
    combine_for(back_order[0])
    for step, distance in enumerate(back_order):
        combine_for(distance)
        for h in range(2):
            for way in range(2):
                if distance > reach[way]:
                    continue
                total = partial[block(way, distance), halves[h]]
                got = arrived(way, distance, h)
                if got is not None:
                    total = total + got
                sums_out[way, distance - 1, :, halves[h]] = total.astype(BF16)
                copy = sum_copy(way, distance, h)
                copy.start()
                pending.append(copy)
        for ahead in back_order[step + 1 : step + 3]:
            combine_for(ahead)
        turn, off = divmod(step - first_add, add_every)
        if off == 0 and 0 <= turn < chips:
            pair_add(chip_order[turn])
    for c in range(chunks):
        if c not in combined:
            combine(c)

    summed = paired[0].astype(F32)
    for d in range(1, chips):
        cross_copy(d).wait_recv()
        summed = summed + crossed[d - 1].astype(F32)
    summed = summed.astype(BF16)
    for i, out in enumerate((grad_gate, grad_up)):
        for e in range(local):
            low = (i * local + e) * part
            out[e] = summed[low : low + part]
    low = 2 * local * part
    for e in range(local):
        grad_down[e] = summed[low : low + ff, e * part : (e + 1) * part]

    for h, low in ((0, 0), (1, middle)):
        total = partial[0:ROWS, halves[h]] + arrived(0, 0, h) + arrived(1, 0, h)
        for out, begin, size in ((mixed, 0, width), (grad_tokens, width, width), (grad_route, 2 * width, LANES)):
            start, stop = max(begin, low), min(begin + size, low + total.shape[1])
            if start < stop:
                value = total[:, start - low : stop - low]
                if size == LANES:
                    out[...] = value[:, 0:top]
                else:
                    out[:, start - begin : stop - begin] = value.astype(BF16)

    for copy in pending:
        copy.wait_send()


def copy_out(*refs):
    count = len(refs) // 2
    for source, target in zip(refs[:count], refs[count:]):
        target[...] = source[...]


def per_device(tokens, out_grad, expert_ids, route_weight, gate_weight, up_weight, down_weight):
    width = tokens.shape[1]
    top = expert_ids.shape[1]
    local, _, ff = gate_weight.shape
    nodes = lax.axis_size("node")
    inners = lax.axis_size("inner")
    reps = lax.axis_size("rep")
    chips = reps // 2
    part = width // reps
    lanes = 2 * width + LANES
    chunks = nodes // GROUP
    half = nodes // 2
    slice_shape = (2 * local * part + ff, ff)
    count = nodes * ROWS
    vmem = pl.BlockSpec(memory_space=pltpu.VMEM)
    anywhere = pl.BlockSpec(memory_space=pl.ANY)
    dma = pltpu.SemaphoreType.DMA
    others = max(1, chips - 1)
    results = pl.pallas_call(
        functools.partial(kernel, (nodes, inners, chips, width, ff, top, local)),
        out_shape=(
            jax.ShapeDtypeStruct((ROWS, width), BF16),
            jax.ShapeDtypeStruct((ROWS, width), BF16),
            jax.ShapeDtypeStruct((ROWS, top), F32),
            jax.ShapeDtypeStruct((local, part, ff), BF16),
            jax.ShapeDtypeStruct((local, part, ff), BF16),
            jax.ShapeDtypeStruct((local, ff, part), BF16),
        ),
        in_specs=[vmem] * 4 + [anywhere] * 3,
        out_specs=[vmem] * 6,
        scratch_shapes=[
            pltpu.VMEM((2, ROWS, LANES), F32),
            pltpu.VMEM((count, lanes), BF16),
            pltpu.VMEM((chunks, inners * ROWS, GROUP * ROWS), F32),
            pltpu.VMEM((chunks, inners, ROWS, lanes), BF16),
            pltpu.VMEM((chunks, inners, ROWS, lanes), BF16),
            pltpu.VMEM((chunks, inners, ROWS, lanes), BF16),
            pltpu.VMEM((chunks, inners, ROWS, lanes), BF16),
            pltpu.VMEM((count, lanes), F32),
            pltpu.VMEM((2, half, ROWS, lanes), BF16),
            pltpu.VMEM((2, half, ROWS, lanes), BF16),
            pltpu.VMEM(gate_weight.shape, BF16),
            pltpu.VMEM(up_weight.shape, BF16),
            pltpu.VMEM(down_weight.shape, BF16),
            pltpu.VMEM((2, chips) + slice_shape, BF16),
            pltpu.VMEM((chips,) + slice_shape, BF16),
            pltpu.VMEM((others,) + slice_shape, BF16),
            dma((3,)),
            dma((2, half, 2)),
            dma((2, half, 2)),
            dma((chunks, inners)),
            dma((chunks, inners)),
            dma((chunks, inners)),
            dma((chunks, inners)),
            dma((2, half, 2)),
            dma((2, half, 2)),
            dma((chips,)),
            dma((chips,)),
            dma((others,)),
            dma((others,)),
        ],
        compiler_params=pltpu.CompilerParams(
            collective_id=0, has_side_effects=True, vmem_limit_bytes=56 * 1024 * 1024
        ),
        cost_estimate=pl.CostEstimate(
            flops=2 * 9 * local * count // ROWS * inners * width * ff,
            bytes_accessed=12 * local * width * ff,
            transcendentals=local * count * ff,
        ),
    )(tokens, out_grad, expert_ids, route_weight, gate_weight, up_weight, down_weight)
    shapes = [jax.ShapeDtypeStruct(result.shape, result.dtype) for result in results]
    return pl.pallas_call(
        copy_out, out_shape=shapes, in_specs=[vmem] * len(results), out_specs=[vmem] * len(results)
    )(*results)


def solution(mesh):
    split = P(("node", "inner", "rep"), None)
    held = P(("node", "inner"), None, None)
    return jax.shard_map(
        per_device,
        mesh=mesh,
        in_specs=(split,) * 4 + (held,) * 3,
        out_specs=(split,) * 3
        + (P(("node", "inner"), "rep", None),) * 2
        + (P(("node", "inner"), None, "rep"),),
        check_vma=False,
    )
```
